32 devices in a mesh: groups: 2 (over y), dp: 4 (over z), pipe: 2 (over core), tensor: 2 (over x).
Axes of the slice: x: 2, y: 2, z: 4, core: 2. Of those that a mesh axis runs over, the one named last changes fastest.
Arguments:
- layer_inputs: bfloat16 [2, 4096, 5120], P('pipe', ('groups', 'dp'), 'tensor'), parts along dimension 1, may hold values from -6 to 6
- output_grads: bfloat16 [2, 4096, 5120], P('pipe', ('groups', 'dp', 'tensor')), parts along dimension 1, may hold values from -6 to 6
- proj_in: bfloat16 [2, 64, 5120], P('pipe', None, 'tensor'), may hold values from -0.078125 to 0.078125
- proj_out: bfloat16 [2, 64, 5120], P('pipe'), may hold values from -0.078125 to 0.078125
- counts: int32 [8], P(('groups', 'dp')), parts along dimension 0, may hold values from 1 to 512, 1536 in all
- token_mask: int32 [4096], P(('groups', 'dp')), parts along dimension 0, may hold values 0 or 1
- precond_out: float32 [2, 64, 64], P('pipe'), may hold values from -1 to 3
- precond_in: float32 [2, 64, 64], P('pipe'), may hold values from -1 to 3
- queries: bfloat16 [256, 2, 64, 64], P('dp', 'pipe', 'tensor'), may hold values from -0.0029296875 to 0.0029296875
- query_ids: int32 [512], P(('groups', 'dp', 'pipe', 'tensor')), parts along dimension 0, may hold values from -1 to 3, as said below
Outputs:
- scores: float32 [256, 8], P(('dp', 'pipe', 'tensor'), 'groups'), parts along dimension 1
The draws below stay inside these ranges and needn't reach their ends.
There are 2 independent parts, one for each index of `groups`. The reference program is written for one: setup_inputs(seed, part) draws one part's arguments, and reference() takes and returns one part's arrays. A program takes and returns all parts, laid end to end along the dimension named above; an argument that names none is the same for every part. Nothing has to cross between parts.
Inputs may be any that keep to these rules, and one draw needn't show every extreme that they name: `counts`: the 4 entries of one group sum to 1536. `query_ids`: about half of the entries are -1.
All inputs are finite; a program needn't handle non-finite values. No bound on the sum of `token_mask` on one device may be relied on, other than what follows from the above.
Results may differ from the reference program's by a relative error of at most 0.003.
Values may be sent and summed in bfloat16 or wider, within the bound.
A program may use at most 64 MiB of HBM per device.

```python
import math
import jax
import jax.numpy as jnp
import numpy as np
from jax import lax

D = 5120
RANK = 64
SEQ = 512
EXAMPLES = 4
TOKENS = 2048
NQ = 256
LAYERS = 2


def draw_precond_out(key, part):
    key = jax.random.fold_in(key, 11)
    first, second = jax.random.split(key)
    spread = jax.random.normal(second, (LAYERS, RANK, RANK), jnp.float32) * (0.6 / math.sqrt(RANK))
    scale = jnp.exp(jax.random.uniform(first, (LAYERS, RANK), jnp.float32, -0.7, 0.7))
    eye = jnp.eye(RANK, dtype=jnp.float32)
    return spread + eye[None, :, :] * scale[:, :, None]


def draw_precond_in(key, part):
    key = jax.random.fold_in(key, 23)
    first, second = jax.random.split(key)
    spread = jax.random.normal(second, (LAYERS, RANK, RANK), jnp.float32) * (0.6 / math.sqrt(RANK))
    scale = jnp.exp(jax.random.uniform(first, (LAYERS, RANK), jnp.float32, -0.7, 0.7))
    eye = jnp.eye(RANK, dtype=jnp.float32)
    return spread + eye[None, :, :] * scale[:, :, None]


def draw_query_ids(key, part):
    key = jax.random.fold_in(key, 37)
    first, second = jax.random.split(key)
    picked = jax.random.randint(first, (NQ,), 0, EXAMPLES, dtype=jnp.int32)
    picked = picked.at[0].set(EXAMPLES - 1)
    keeper = jax.random.randint(second, (NQ,), 0, 2, dtype=jnp.int32)
    keeper = keeper.at[0].set(1)
    keeper = keeper.at[1].set(0)
    return jnp.where(keeper == 1, picked, -1).astype(jnp.int32)


def touch_ends(array, key, least, largest):
    dims = array.shape
    place = [jax.random.randint(jax.random.fold_in(key, axis), (), 0, dims[axis]) for axis in range(len(dims))]
    array = array.at[tuple(place)].set(least)
    longest = dims.index(max(dims))
    place[longest] = (place[longest] + 1) % dims[longest]
    return array.at[tuple(place)].set(largest)


def block_scale(key, dims, cuts, least, top_value):
    def one(axis_at, shards_of):
        steps = jax.random.uniform(jax.random.fold_in(jax.random.fold_in(key, 6), axis_at), (shards_of,), jnp.float32, least / len(cuts), top_value / len(cuts))
        return jnp.repeat(jnp.exp(steps), dims[axis_at] // shards_of).reshape((-1,) + (1,) * (len(dims) - axis_at - 1))

    loudness = one(*cuts[0])
    for cut in cuts[1:]:
        loudness = loudness * one(*cut)
    return loudness


def profile(count, total, reach, slope):
    weights = [(1 << 20) // math.isqrt(grade ** slope) + 1 for grade in range(2, count + 1)]
    rest, holding = total - reach - (count - 1), [1] * (count - 1)
    while rest > 0:
        candidates = [i for i in range(count - 1) if holding[i] < reach]
        whole, remaining = sum([weights[i] for i in candidates]), rest
        for i in candidates:
            addition = min(reach - holding[i], max(1, remaining * weights[i] // whole), rest)
            holding[i] = holding[i] + addition
            rest = rest - addition
    return np.array([reach] + holding)


def ragged(key, count, total, reach, slope):
    if count == 2:
        one = jax.random.randint(key, (), max(1, total - reach), min(reach, total - 1) + 1)
        return jnp.stack([one, total - one])
    tallies = jnp.asarray(profile(count, total, reach, slope), jnp.int32)
    pairs = (count - 1) // 2
    donor, receiver = tallies[1:1 + 2 * pairs:2], tallies[2:2 + 2 * pairs:2]
    slack = jnp.minimum(donor - 1, reach - receiver)
    shifted = jax.random.randint(jax.random.fold_in(key, 1), (pairs,), 0, 1 << 20) % (slack + 1)
    tallies = tallies.at[1:1 + 2 * pairs:2].set(donor - shifted).at[2:2 + 2 * pairs:2].set(receiver + shifted)
    return tallies[jax.random.permutation(jax.random.fold_in(key, 2), count)]


def noise(own_key, shape, deviation, most, pieces=(), kind=jnp.bfloat16):
    result = deviation * jax.random.normal(own_key, shape, jnp.float32)
    if pieces:
        result = result * block_scale(own_key, shape, pieces, -0.22, 0.18)
    return jnp.clip(result, -most, most).astype(kind)


def setup_inputs(seed: int = 0, part: int = 0) -> dict:
    arg_keys = jax.random.split(jax.random.key(seed), 11)
    part_keys = jax.random.split(jax.random.fold_in(arg_keys[10], part), 11)
    layer_inputs = noise(part_keys[0], (LAYERS, TOKENS, D), 1.0, 6.0, ((0, 2), (1, 4), (2, 2)))
    output_grads = noise(part_keys[1], (LAYERS, TOKENS, D), 1.0, 6.0, ((0, 2), (1, 8)))
    proj_in = noise(arg_keys[2], (LAYERS, RANK, D), D ** -0.5, 0.078125, ((0, 2), (2, 2)))
    proj_out = noise(arg_keys[3], (LAYERS, RANK, D), D ** -0.5, 0.078125, ((0, 2),))
    counts = ragged(part_keys[4], EXAMPLES, EXAMPLES * SEQ * 3 // 4, SEQ, 1).astype(jnp.int32)
    token_mask = touch_ends((jax.random.randint(part_keys[5], (TOKENS,), 0, 4) < 3).astype(jnp.int32), jax.random.fold_in(part_keys[5], 1), 0, 1)
    precond_out = draw_precond_out(jax.random.fold_in(arg_keys[10], 71), part)
    precond_in = draw_precond_in(jax.random.fold_in(arg_keys[10], 71), part)
    queries = noise(arg_keys[8], (NQ, LAYERS, RANK, RANK), (LAYERS * RANK * RANK * SEQ) ** -0.5, 0.0029296875, ((0, 4), (1, 2), (2, 2)))
    query_ids = draw_query_ids(jax.random.fold_in(jax.random.fold_in(arg_keys[10], part), 71), part)
    return dict(layer_inputs=layer_inputs, output_grads=output_grads, proj_in=proj_in, proj_out=proj_out, counts=counts, token_mask=token_mask, precond_out=precond_out, precond_in=precond_in, queries=queries, query_ids=query_ids)


def reference(layer_inputs, output_grads, proj_in, proj_out, counts, token_mask, precond_out, precond_in, queries, query_ids):
    highest = lax.Precision.HIGHEST
    slots = jnp.arange(TOKENS, dtype=jnp.int32)
    position = slots % SEQ
    owner = slots // SEQ
    limit = counts[owner]
    weight = jnp.where((position < limit) & (token_mask == 1), 1.0, 0.0).astype(jnp.float32)
    stacked = []
    for layer in range(LAYERS):
        in_proj = jnp.dot(layer_inputs[layer], proj_in[layer].T, preferred_element_type=jnp.float32)
        out_proj = jnp.dot(output_grads[layer], proj_out[layer].T, preferred_element_type=jnp.float32)
        weighted = (out_proj * weight[:, None]).reshape(EXAMPLES, SEQ, RANK)
        grads = jnp.einsum("esr,esc->erc", weighted, in_proj.reshape(EXAMPLES, SEQ, RANK), precision=highest)
        left = jnp.einsum("ab,ebc->eac", precond_out[layer], grads, precision=highest)
        precond = jnp.einsum("eac,cd->ead", left, precond_in[layer], precision=highest).astype(jnp.bfloat16)
        stacked.append(precond.reshape(EXAMPLES, RANK * RANK))
    train_flat = jnp.concatenate(stacked, axis=1)
    query_flat = queries.reshape(NQ, LAYERS * RANK * RANK)
    scores = jnp.dot(query_flat, train_flat.T, preferred_element_type=jnp.float32)
    hits = query_ids[:, None] == jnp.arange(EXAMPLES, dtype=jnp.int32)[None, :]
    return jnp.where(hits, 0.0, scores).astype(jnp.float32)
```

```python
import functools

import jax
import jax.numpy as jnp
from jax import lax
from jax.experimental import pallas as pl
from jax.experimental.pallas import tpu as pltpu
from jax.sharding import PartitionSpec as P

MESH = pl.DeviceIdType.MESH
HIGHEST = lax.Precision.HIGHEST
NT = (((1,), (1,)), ((), ()))


def dot_nt(a, b, precision=None):
    return lax.dot_general(a, b, NT, precision=precision, preferred_element_type=jnp.float32)


def kernel(
    dims,
    x_hbm,
    g_hbm,
    pin_hbm,
    pout_hbm,
    counts_hbm,
    mask_hbm,
    left_hbm,
    right_hbm,
    q_hbm,
    out_ref,
    x_v,
    g_v,
    pin_v,
    pout_v,
    count_s,
    mask_v,
    left_v,
    right_v,
    q_v,
    outs,
    p_send,
    p_recv,
    s_send,
    s_recv,
    load_sem,
    x_sem,
    g_sem,
    a_send_sem,
    a_recv_sem,
    b_send_sem,
    b_recv_sem,
    c_send_sem,
    c_recv_sem,
):
    dp, pipe, tensor, x_chunks, g_chunks = dims
    d, p, t = lax.axis_index("dp"), lax.axis_index("pipe"), lax.axis_index("tensor")
    rank = pout_v.shape[0]
    own_tok = g_v.shape[0]
    rows = rank // tensor
    nq = q_v.shape[0]

    def shift(i, by, size):
        return lax.rem(i + by, size)

    load_pout = pltpu.make_async_copy(pout_hbm.at[0], pout_v, load_sem.at[0])
    load_pout.start()
    g_loads = []
    g_width = g_v.shape[1] // g_chunks
    for c in range(g_chunks):
        cols = pl.ds(c * g_width, g_width)
        load = pltpu.make_async_copy(g_hbm.at[0, :, cols], g_v.at[:, cols], g_sem.at[c])
        load.start()
        g_loads.append(load)
    load_count = pltpu.make_async_copy(counts_hbm, count_s, load_sem.at[1])
    load_mask = pltpu.make_async_copy(mask_hbm, mask_v, load_sem.at[2])
    load_pin = pltpu.make_async_copy(pin_hbm.at[0], pin_v, load_sem.at[3])
    load_count.start()
    load_mask.start()
    load_pin.start()
    x_loads = []
    x_width = x_v.shape[1] // x_chunks
    for c in range(x_chunks):
        cols = pl.ds(c * x_width, x_width)
        load = pltpu.make_async_copy(x_hbm.at[0, :, cols], x_v.at[:, cols], x_sem.at[c])
        load.start()
        x_loads.append(load)
    load_left = pltpu.make_async_copy(left_hbm.at[0], left_v, load_sem.at[4])
    load_right = pltpu.make_async_copy(right_hbm.at[0], right_v, load_sem.at[5])
    load_q = pltpu.make_async_copy(q_hbm.at[:, 0], q_v, load_sem.at[6])
    load_left.start()
    load_right.start()
    load_q.start()

    barrier = pltpu.get_barrier_semaphore()
    block_peers = [(i, j) for i in range(dp) for j in range(tensor) if (i, j) != (0, 0)]
    score_peers = [(i, j) for i in range(pipe) for j in range(tensor) if (i, j) != (0, 0)]
    met = 0
    for i, j in block_peers:
        pl.semaphore_signal(
            barrier, inc=1, device_id={"dp": shift(d, i, dp), "tensor": shift(t, j, tensor)}, device_id_type=MESH
        )
        met += 1
    for i, j in score_peers:
        if i:
            pl.semaphore_signal(
                barrier, inc=1, device_id={"pipe": shift(p, i, pipe), "tensor": shift(t, j, tensor)}, device_id_type=MESH
            )
            met += 1

    load_pout.wait()
    total = jnp.zeros((rank, own_tok), jnp.float32)
    for c in range(g_chunks):
        g_loads[c].wait()
        cols = slice(c * g_width, (c + 1) * g_width)
        total += dot_nt(pout_v[:, cols], g_v[:, cols])
    load_count.wait()
    load_mask.wait()
    start = pl.multiple_of(t * own_tok, own_tok)
    position = start + lax.broadcasted_iota(jnp.int32, (1, own_tok), 1)
    keep = (position < count_s[0]) & (mask_v[:, pl.ds(start, own_tok)] == 1)
    outs[t] = jnp.where(keep, total, 0.0)

    pl.semaphore_wait(barrier, met)
    a_copies = []
    for j in range(1, tensor):
        copy = pltpu.make_async_remote_copy(
            src_ref=outs.at[t],
            dst_ref=outs.at[t],
            send_sem=a_send_sem.at[j],
            recv_sem=a_recv_sem.at[t],
            device_id={"tensor": shift(t, j, tensor)},
            device_id_type=MESH,
        )
        copy.start()
        a_copies.append(copy)

    load_pin.wait()
    ins = jnp.zeros((rank, x_v.shape[0]), jnp.float32)
    for c in range(x_chunks):
        x_loads[c].wait()
        cols = slice(c * x_width, (c + 1) * x_width)
        ins += dot_nt(pin_v[:, cols], x_v[:, cols])
    load_left.wait()
    load_right.wait()
    for j in range(1, tensor):
        source = shift(t, j, tensor)
        pltpu.make_async_remote_copy(
            src_ref=outs.at[source],
            dst_ref=outs.at[source],
            send_sem=a_send_sem.at[j],
            recv_sem=a_recv_sem.at[source],
            device_id={"tensor": source},
            device_id_type=MESH,
        ).wait_recv()
    grads = jnp.zeros((rank, rank), jnp.float32)
    for j in range(tensor):
        grads += dot_nt(outs[j], ins[:, j * own_tok : (j + 1) * own_tok], HIGHEST)
    half = jnp.dot(left_v[...], grads, precision=HIGHEST, preferred_element_type=jnp.float32)
    block = jnp.dot(half, right_v[...], precision=HIGHEST, preferred_element_type=jnp.float32)
    p_send[...] = block.reshape(tensor, rows, rank)

    b_copies = []
    for i, j in block_peers:
        other = shift(t, j, tensor)
        copy = pltpu.make_async_remote_copy(
            src_ref=p_send.at[other],
            dst_ref=p_recv.at[d, t],
            send_sem=b_send_sem.at[i, j],
            recv_sem=b_recv_sem.at[d, t],
            device_id={"dp": shift(d, i, dp), "tensor": other},
            device_id_type=MESH,
        )
        copy.start()
        b_copies.append(copy)
    p_recv[d, t] = p_send[t]
    load_q.wait()
    for i, j in block_peers:
        from_d, from_t = shift(d, i, dp), shift(t, j, tensor)
        pltpu.make_async_remote_copy(
            src_ref=p_send.at[from_t],
            dst_ref=p_recv.at[from_d, from_t],
            send_sem=b_send_sem.at[i, j],
            recv_sem=b_recv_sem.at[from_d, from_t],
            device_id={"dp": from_d, "tensor": from_t},
            device_id_type=MESH,
        ).wait_recv()
    precond = p_recv[:, 0]
    for j in range(1, tensor):
        precond += p_recv[:, j]
    precond = precond.astype(jnp.bfloat16).reshape(dp * rows, rank)

    lanes = dp * rows
    products = dot_nt(q_v[...].reshape(nq * rows, rank), precond).reshape(nq, rows, lanes)
    row = lax.broadcasted_iota(jnp.int32, (rows, lanes), 0)
    lane = lax.broadcasted_iota(jnp.int32, (rows, lanes), 1)
    same = (lax.rem(lane, rows) == row)[None]
    sums = jnp.sum(jnp.where(same, products, 0.0), axis=1)
    s_send[...] = sums.reshape(s_send.shape)

    mine = p * tensor + t
    c_copies = []
    for i, j in score_peers:
        to_p, to_t = shift(p, i, pipe), shift(t, j, tensor)
        copy = pltpu.make_async_remote_copy(
            src_ref=s_send.at[to_p * tensor + to_t],
            dst_ref=s_recv.at[mine],
            send_sem=c_send_sem.at[i, j],
            recv_sem=c_recv_sem.at[mine],
            device_id={"pipe": to_p, "tensor": to_t},
            device_id_type=MESH,
        )
        copy.start()
        c_copies.append(copy)
    s_recv[mine] = s_send[mine]
    for i, j in score_peers:
        from_p, from_t = shift(p, i, pipe), shift(t, j, tensor)
        source = from_p * tensor + from_t
        pltpu.make_async_remote_copy(
            src_ref=s_send.at[source],
            dst_ref=s_recv.at[source],
            send_sem=c_send_sem.at[i, j],
            recv_sem=c_recv_sem.at[source],
            device_id={"pipe": from_p, "tensor": from_t},
            device_id_type=MESH,
        ).wait_recv()
    scores = s_recv[0]
    for i in range(1, pipe * tensor):
        scores += s_recv[i]
    owner = lax.broadcasted_iota(jnp.int32, (dp, lanes), 0)
    lane = lax.broadcasted_iota(jnp.int32, (dp, lanes), 1)
    gather = jnp.where(lax.div(lane, rows) == owner, 1.0, 0.0).astype(jnp.float32)
    out_ref[...] = dot_nt(gather, scores, HIGHEST)
    for copy in a_copies + b_copies + c_copies:
        copy.wait_send()


def cut(width):
    return max(n for n in (1, 2, 3, 4) if width % (n * 128) == 0)


def local(mesh, *args):
    x, g, pin, pout, counts, mask, left, right, queries, query_ids = args
    dp, pipe, tensor = mesh.shape["dp"], mesh.shape["pipe"], mesh.shape["tensor"]
    rank = pin.shape[1]
    rows = rank // tensor
    nq = queries.shape[0]
    parts = pipe * tensor
    lanes = dp * rows
    x_chunks, g_chunks = cut(x.shape[2]), cut(g.shape[2])
    f32, bf16 = jnp.float32, jnp.bfloat16
    hbm = pl.BlockSpec(memory_space=pltpu.HBM)
    dma = pltpu.SemaphoreType.DMA
    scores = pl.pallas_call(
        functools.partial(kernel, (dp, pipe, tensor, x_chunks, g_chunks)),
        out_shape=jax.ShapeDtypeStruct((dp, nq // parts), f32),
        in_specs=[hbm] * 9,
        out_specs=pl.BlockSpec(memory_space=pltpu.VMEM),
        scratch_shapes=[
            pltpu.VMEM(x.shape[1:], bf16),
            pltpu.VMEM(g.shape[1:], bf16),
            pltpu.VMEM(pin.shape[1:], bf16),
            pltpu.VMEM(pout.shape[1:], bf16),
            pltpu.SMEM(counts.shape, jnp.int32),
            pltpu.VMEM((1, mask.shape[0]), jnp.int32),
            pltpu.VMEM((rank, rank), f32),
            pltpu.VMEM((rank, rank), f32),
            pltpu.VMEM((nq, rows, rank), bf16),
            pltpu.VMEM((tensor, rank, g.shape[1]), f32),
            pltpu.VMEM((tensor, rows, rank), f32),
            pltpu.VMEM((dp, tensor, rows, rank), f32),
            pltpu.VMEM((parts, nq // parts, lanes), f32),
            pltpu.VMEM((parts, nq // parts, lanes), f32),
            dma((7,)),
            dma((x_chunks,)),
            dma((g_chunks,)),
            dma((tensor,)),
            dma((tensor,)),
            dma((dp, tensor)),
            dma((dp, tensor)),
            dma((pipe, tensor)),
            dma((parts,)),
        ],
        compiler_params=pltpu.CompilerParams(
            collective_id=0, has_side_effects=True, vmem_limit_bytes=60 * 1024 * 1024
        ),
        name="attribution",
    )(x, g, pin, pout, counts, mask.reshape(1, -1), left, right, queries)
    hits = query_ids[None, :] == jnp.arange(dp, dtype=jnp.int32)[:, None]
    return jnp.where(hits, 0.0, scores).T


def solution(mesh):
    placed = (
        P("pipe", ("groups", "dp"), "tensor"),
        P("pipe", ("groups", "dp", "tensor"), None),
        P("pipe", None, "tensor"),
        P("pipe", None, None),
        P(("groups", "dp")),
        P(("groups", "dp")),
        P("pipe", None, None),
        P("pipe", None, None),
        P("dp", "pipe", "tensor", None),
        P(("groups", "dp", "pipe", "tensor")),
    )
    return jax.shard_map(
        functools.partial(local, mesh),
        mesh=mesh,
        in_specs=placed,
        out_specs=P(("dp", "pipe", "tensor"), "groups"),
        check_vma=False,
    )
```

```python
import functools

import jax
import jax.numpy as jnp
from jax import lax
from jax.experimental import pallas as pl
from jax.experimental.pallas import tpu as pltpu
from jax.sharding import PartitionSpec as P

MESH = pl.DeviceIdType.MESH
HIGHEST = lax.Precision.HIGHEST
NT = (((1,), (1,)), ((), ()))


def dot_nt(a, b, precision=None):
    return lax.dot_general(a, b, NT, precision=precision, preferred_element_type=jnp.float32)


def kernel(
    dims,
    x_hbm,
    g_hbm,
    pin_hbm,
    pout_hbm,
    counts_hbm,
    mask_hbm,
    left_hbm,
    right_hbm,
    q_hbm,
    out_ref,
    x_v,
    g_v,
    pin_v,
    pout_v,
    count_s,
    mask_v,
    left_v,
    right_v,
    q_v,
    q_send,
    q_recv,
    outs,
    p_send,
    p_recv,
    s_send,
    s_recv,
    load_sem,
    x_sem,
    g_sem,
    a_send_sem,
    a_recv_sem,
    b_send_sem,
    b_recv_sem,
    q_send_sem,
    q_recv_sem,
    c_send_sem,
    c_recv_sem,
):
    dp, pipe, tensor, x_chunks, g_chunks = dims
    d, p, t = lax.axis_index("dp"), lax.axis_index("pipe"), lax.axis_index("tensor")
    rank = pout_v.shape[0]
    own_tok = g_v.shape[0]
    rows = rank // tensor
    nq = q_v.shape[0] // (pipe * tensor)
    pairs = rows // 2

    def shift(i, by, size):
        return lax.rem(i + by, size)

    load_pout = pltpu.make_async_copy(pout_hbm.at[0], pout_v, load_sem.at[0])
    load_pout.start()
    g_loads = []
    g_width = g_v.shape[1] // g_chunks
    for c in range(g_chunks):
        cols = pl.ds(c * g_width, g_width)
        load = pltpu.make_async_copy(g_hbm.at[0, :, cols], g_v.at[:, cols], g_sem.at[c])
        load.start()
        g_loads.append(load)
    load_count = pltpu.make_async_copy(counts_hbm, count_s, load_sem.at[1])
    load_mask = pltpu.make_async_copy(mask_hbm, mask_v, load_sem.at[2])
    load_pin = pltpu.make_async_copy(pin_hbm.at[0], pin_v, load_sem.at[3])
    load_count.start()
    load_mask.start()
    load_pin.start()
    load_q = pltpu.make_async_copy(q_hbm.at[:, 0], q_v, load_sem.at[6])
    load_q.start()
    x_loads = []
    x_width = x_v.shape[1] // x_chunks
    for c in range(x_chunks):
        cols = pl.ds(c * x_width, x_width)
        load = pltpu.make_async_copy(x_hbm.at[0, :, cols], x_v.at[:, cols], x_sem.at[c])
        load.start()
        x_loads.append(load)
    load_left = pltpu.make_async_copy(left_hbm.at[0], left_v, load_sem.at[4])
    load_right = pltpu.make_async_copy(right_hbm.at[0], right_v, load_sem.at[5])
    load_left.start()
    load_right.start()

    barrier = pltpu.get_barrier_semaphore()
    block_peers = [(i, j) for i in range(dp) for j in range(tensor) if (i, j) != (0, 0)]
    met = 0
    for i, j in block_peers:
        pl.semaphore_signal(
            barrier, inc=1, device_id={"dp": shift(d, i, dp), "tensor": shift(t, j, tensor)}, device_id_type=MESH
        )
        met += 1
    for i in range(1, pipe):
        pl.semaphore_signal(barrier, inc=1, device_id={"pipe": shift(p, i, pipe)}, device_id_type=MESH)
        met += 1

    load_pout.wait()
    total = jnp.zeros((rank, own_tok), jnp.float32)
    for c in range(g_chunks):
        g_loads[c].wait()
        cols = slice(c * g_width, (c + 1) * g_width)
        total += dot_nt(pout_v[:, cols], g_v[:, cols])
    load_count.wait()
    load_mask.wait()
    start = pl.multiple_of(t * own_tok, own_tok)
    position = start + lax.broadcasted_iota(jnp.int32, (1, own_tok), 1)
    keep = (position < count_s[0]) & (mask_v[:, pl.ds(start, own_tok)] == 1)
    outs[t] = jnp.where(keep, total, 0.0)

    pl.semaphore_wait(barrier, met)
    a_copies = []
    for j in range(1, tensor):
        copy = pltpu.make_async_remote_copy(
            src_ref=outs.at[t],
            dst_ref=outs.at[t],
            send_sem=a_send_sem.at[j],
            recv_sem=a_recv_sem.at[t],
            device_id={"tensor": shift(t, j, tensor)},
            device_id_type=MESH,
        )
        copy.start()
        a_copies.append(copy)

    load_q.wait()

    def packed(owner):
        parts = [q_v[pl.ds((i * tensor + owner) * nq, nq)] for i in range(pipe)]
        both = jnp.concatenate(parts, axis=0)
        both = jnp.concatenate([both[:, :pairs], both[:, pairs:]], axis=-1)
        return both.reshape(q_send.shape[1:])

    for j in range(1, tensor):
        other = shift(t, j, tensor)
        q_send[other] = packed(other)
        copy = pltpu.make_async_remote_copy(
            src_ref=q_send.at[other],
            dst_ref=q_recv.at[t],
            send_sem=q_send_sem.at[j],
            recv_sem=q_recv_sem.at[t],
            device_id={"tensor": other},
            device_id_type=MESH,
        )
        copy.start()
        a_copies.append(copy)
    q_recv[t] = packed(t)

    load_pin.wait()
    ins = jnp.zeros((rank, x_v.shape[0]), jnp.float32)
    for c in range(x_chunks):
        x_loads[c].wait()
        cols = slice(c * x_width, (c + 1) * x_width)
        ins += dot_nt(pin_v[:, cols], x_v[:, cols])
    load_left.wait()
    load_right.wait()
    for j in range(1, tensor):
        source = shift(t, j, tensor)
        pltpu.make_async_remote_copy(
            src_ref=outs.at[source],
            dst_ref=outs.at[source],
            send_sem=a_send_sem.at[j],
            recv_sem=a_recv_sem.at[source],
            device_id={"tensor": source},
            device_id_type=MESH,
        ).wait_recv()
    grads = jnp.zeros((rank, rank), jnp.float32)
    for j in range(tensor):
        grads += dot_nt(outs[j], ins[:, j * own_tok : (j + 1) * own_tok], HIGHEST)
    half = jnp.dot(left_v[...], grads, precision=HIGHEST, preferred_element_type=jnp.float32)
    block = jnp.dot(half, right_v[...], precision=HIGHEST, preferred_element_type=jnp.float32)
    block = block.reshape(tensor, 2, pairs, rank)
    p_send[...] = jnp.concatenate([block[:, 0], block[:, 1]], axis=-1)

    b_copies = []
    for i, j in block_peers:
        other = shift(t, j, tensor)
        copy = pltpu.make_async_remote_copy(
            src_ref=p_send,
            dst_ref=p_recv.at[d, t],
            send_sem=b_send_sem.at[i, j],
            recv_sem=b_recv_sem.at[d, t],
            device_id={"dp": shift(d, i, dp), "tensor": other},
            device_id_type=MESH,
        )
        copy.start()
        b_copies.append(copy)
    p_recv[d, t] = p_send[...]
    for j in range(1, tensor):
        source = shift(t, j, tensor)
        pltpu.make_async_remote_copy(
            src_ref=q_send.at[source],
            dst_ref=q_recv.at[source],
            send_sem=q_send_sem.at[j],
            recv_sem=q_recv_sem.at[source],
            device_id={"tensor": source},
            device_id_type=MESH,
        ).wait_recv()
    for i, j in block_peers:
        from_d, from_t = shift(d, i, dp), shift(t, j, tensor)
        pltpu.make_async_remote_copy(
            src_ref=p_send,
            dst_ref=p_recv.at[from_d, from_t],
            send_sem=b_send_sem.at[i, j],
            recv_sem=b_recv_sem.at[from_d, from_t],
            device_id={"dp": from_d, "tensor": from_t},
            device_id_type=MESH,
        ).wait_recv()
    precond = p_recv[:, 0]
    for j in range(1, tensor):
        precond += p_recv[:, j]
    lanes = dp * pairs
    products = jnp.zeros((pipe * nq * pairs, lanes), jnp.float32)
    for j in range(tensor):
        share = precond[:, j].reshape(lanes, 2 * rank).astype(jnp.bfloat16)
        products += dot_nt(q_recv[j], share)
    products = products.reshape(pipe * nq, pairs, lanes)
    row = lax.broadcasted_iota(jnp.int32, (pairs, lanes), 0)
    lane = lax.broadcasted_iota(jnp.int32, (pairs, lanes), 1)
    same = (lax.rem(lane, pairs) == row)[None]
    sums = jnp.sum(jnp.where(same, products, 0.0), axis=1)
    s_send[...] = sums.reshape(s_send.shape)

    c_copies = []
    for i in range(1, pipe):
        other = shift(p, i, pipe)
        copy = pltpu.make_async_remote_copy(
            src_ref=s_send.at[other],
            dst_ref=s_recv.at[p],
            send_sem=c_send_sem.at[i],
            recv_sem=c_recv_sem.at[p],
            device_id={"pipe": other},
            device_id_type=MESH,
        )
        copy.start()
        c_copies.append(copy)
    s_recv[p] = s_send[p]
    for i in range(1, pipe):
        source = shift(p, i, pipe)
        pltpu.make_async_remote_copy(
            src_ref=s_send.at[source],
            dst_ref=s_recv.at[source],
            send_sem=c_send_sem.at[i],
            recv_sem=c_recv_sem.at[source],
            device_id={"pipe": source},
            device_id_type=MESH,
        ).wait_recv()
    scores = s_recv[0]
    for i in range(1, pipe):
        scores += s_recv[i]
    owner = lax.broadcasted_iota(jnp.int32, (dp, lanes), 0)
    lane = lax.broadcasted_iota(jnp.int32, (dp, lanes), 1)
    gather = jnp.where(lax.div(lane, pairs) == owner, 1.0, 0.0).astype(jnp.float32)
    out_ref[...] = dot_nt(gather, scores, HIGHEST)
    for copy in a_copies + b_copies + c_copies:
        copy.wait_send()


def cut(width):
    return max(n for n in (1, 2, 3, 4) if width % (n * 128) == 0)


def local(mesh, *args):
    x, g, pin, pout, counts, mask, left, right, queries, query_ids = args
    dp, pipe, tensor = mesh.shape["dp"], mesh.shape["pipe"], mesh.shape["tensor"]
    rank = pin.shape[1]
    rows = rank // tensor
    nq = queries.shape[0]
    parts = pipe * tensor
    lanes = dp * rows // 2
    x_chunks, g_chunks = cut(x.shape[2]), cut(g.shape[2])
    f32, bf16 = jnp.float32, jnp.bfloat16
    hbm = pl.BlockSpec(memory_space=pltpu.HBM)
    dma = pltpu.SemaphoreType.DMA
    scores = pl.pallas_call(
        functools.partial(kernel, (dp, pipe, tensor, x_chunks, g_chunks)),
        out_shape=jax.ShapeDtypeStruct((dp, nq // parts), f32),
        in_specs=[hbm] * 9,
        out_specs=pl.BlockSpec(memory_space=pltpu.VMEM),
        scratch_shapes=[
            pltpu.VMEM(x.shape[1:], bf16),
            pltpu.VMEM(g.shape[1:], bf16),
            pltpu.VMEM(pin.shape[1:], bf16),
            pltpu.VMEM(pout.shape[1:], bf16),
            pltpu.SMEM(counts.shape, jnp.int32),
            pltpu.VMEM((1, mask.shape[0]), jnp.int32),
            pltpu.VMEM((rank, rank), f32),
            pltpu.VMEM((rank, rank), f32),
            pltpu.VMEM((nq, rows, rank), bf16),
            pltpu.VMEM((tensor, pipe * (nq // parts) * rows // 2, 2 * rank), bf16),
            pltpu.VMEM((tensor, pipe * (nq // parts) * rows // 2, 2 * rank), bf16),
            pltpu.VMEM((tensor, rank, g.shape[1]), f32),
            pltpu.VMEM((tensor, rows // 2, 2 * rank), f32),
            pltpu.VMEM((dp, tensor, tensor, rows // 2, 2 * rank), f32),
            pltpu.VMEM((pipe, nq // parts, lanes), f32),
            pltpu.VMEM((pipe, nq // parts, lanes), f32),
            dma((7,)),
            dma((x_chunks,)),
            dma((g_chunks,)),
            dma((tensor,)),
            dma((tensor,)),
            dma((dp, tensor)),
            dma((dp, tensor)),
            dma((tensor,)),
            dma((tensor,)),
            dma((pipe,)),
            dma((pipe,)),
        ],
        compiler_params=pltpu.CompilerParams(
            collective_id=0, has_side_effects=True, vmem_limit_bytes=60 * 1024 * 1024
        ),
        name="attribution",
    )(x, g, pin, pout, counts, mask.reshape(1, -1), left, right, queries)
    hits = query_ids[None, :] == jnp.arange(dp, dtype=jnp.int32)[:, None]
    return jnp.where(hits, 0.0, scores).T


def solution(mesh):
    placed = (
        P("pipe", ("groups", "dp"), "tensor"),
        P("pipe", ("groups", "dp", "tensor"), None),
        P("pipe", None, "tensor"),
        P("pipe", None, None),
        P(("groups", "dp")),
        P(("groups", "dp")),
        P("pipe", None, None),
        P("pipe", None, None),
        P("dp", "pipe", "tensor", None),
        P(("groups", "dp", "pipe", "tensor")),
    )
    return jax.shard_map(
        functools.partial(local, mesh),
        mesh=mesh,
        in_specs=placed,
        out_specs=P(("dp", "pipe", "tensor"), "groups"),
        check_vma=False,
    )
```

```python
import functools

import jax
import jax.numpy as jnp
from jax import lax
from jax.experimental import pallas as pl
from jax.experimental.pallas import tpu as pltpu
from jax.sharding import PartitionSpec as P

MESH = pl.DeviceIdType.MESH
HIGHEST = lax.Precision.HIGHEST
NT = (((1,), (1,)), ((), ()))


def dot_nt(a, b, precision=None):
    return lax.dot_general(a, b, NT, precision=precision, preferred_element_type=jnp.float32)


def kernel(
    dims,
    x_hbm,
    g_hbm,
    pin_hbm,
    pout_hbm,
    counts_hbm,
    mask_hbm,
    left_hbm,
    right_hbm,
    q_hbm,
    out_ref,
    x_v,
    g_v,
    pin_v,
    pout_v,
    count_s,
    mask_v,
    left_v,
    right_v,
    q_v,
    q_send,
    q_recv,
    outs,
    p_send,
    p_recv,
    s_send,
    s_recv,
    load_sem,
    x_sem,
    g_sem,
    a_send_sem,
    a_recv_sem,
    b_send_sem,
    b_recv_sem,
    q_send_sem,
    q_recv_sem,
    c_send_sem,
    c_recv_sem,
):
    dp, pipe, tensor, x_chunks, g_chunks = dims
    d, p, t = lax.axis_index("dp"), lax.axis_index("pipe"), lax.axis_index("tensor")
    rank = pout_v.shape[0]
    own_tok = g_v.shape[0]
    rows = rank // tensor
    nq = q_v.shape[0] // (pipe * tensor)
    pairs = rows // 2

    def shift(i, by, size):
        return lax.rem(i + by, size)

    barrier = pltpu.get_barrier_semaphore()
    block_peers = [(i, j) for i in range(dp) for j in range(tensor) if (i, j) != (0, 0)]
    met = 0
    for i, j in block_peers:
        pl.semaphore_signal(
            barrier, inc=1, device_id={"dp": shift(d, i, dp), "tensor": shift(t, j, tensor)}, device_id_type=MESH
        )
        met += 1
    for i in range(1, pipe):
        pl.semaphore_signal(barrier, inc=1, device_id={"pipe": shift(p, i, pipe)}, device_id_type=MESH)
        met += 1

    load_pout = pltpu.make_async_copy(pout_hbm.at[0], pout_v, load_sem.at[0])
    load_pout.start()
    g_loads = []
    g_width = g_v.shape[1] // g_chunks
    for c in range(g_chunks):
        cols = pl.ds(c * g_width, g_width)
        load = pltpu.make_async_copy(g_hbm.at[0, :, cols], g_v.at[:, cols], g_sem.at[c])
        load.start()
        g_loads.append(load)
    load_count = pltpu.make_async_copy(counts_hbm, count_s, load_sem.at[1])
    load_mask = pltpu.make_async_copy(mask_hbm, mask_v, load_sem.at[2])
    load_pin = pltpu.make_async_copy(pin_hbm.at[0], pin_v, load_sem.at[3])
    load_count.start()
    load_mask.start()
    load_pin.start()
    load_q = pltpu.make_async_copy(q_hbm.at[:, 0], q_v, load_sem.at[6])
    load_q.start()
    x_loads = []
    x_width = x_v.shape[1] // x_chunks
    for c in range(x_chunks):
        cols = pl.ds(c * x_width, x_width)
        load = pltpu.make_async_copy(x_hbm.at[0, :, cols], x_v.at[:, cols], x_sem.at[c])
        load.start()
        x_loads.append(load)
    load_left = pltpu.make_async_copy(left_hbm.at[0], left_v, load_sem.at[4])
    load_right = pltpu.make_async_copy(right_hbm.at[0], right_v, load_sem.at[5])
    load_left.start()
    load_right.start()

    load_pout.wait()
    total = jnp.zeros((rank, own_tok), jnp.float32)
    for c in range(g_chunks):
        g_loads[c].wait()
        cols = slice(c * g_width, (c + 1) * g_width)
        total += dot_nt(pout_v[:, cols], g_v[:, cols])
    load_count.wait()
    load_mask.wait()
    start = pl.multiple_of(t * own_tok, own_tok)
    position = start + lax.broadcasted_iota(jnp.int32, (1, own_tok), 1)
    keep = (position < count_s[0]) & (mask_v[:, pl.ds(start, own_tok)] == 1)
    outs[t] = jnp.where(keep, total, 0.0)

    pl.semaphore_wait(barrier, met)
    a_copies = []
    for j in range(1, tensor):
        copy = pltpu.make_async_remote_copy(
            src_ref=outs.at[t],
            dst_ref=outs.at[t],
            send_sem=a_send_sem.at[j],
            recv_sem=a_recv_sem.at[t],
            device_id={"tensor": shift(t, j, tensor)},
            device_id_type=MESH,
        )
        copy.start()
        a_copies.append(copy)

    load_q.wait()

    def packed(owner):
        parts = [q_v[pl.ds((i * tensor + owner) * nq, nq)] for i in range(pipe)]
        both = jnp.concatenate(parts, axis=0)
        both = jnp.concatenate([both[:, :pairs], both[:, pairs:]], axis=-1)
        return both.reshape(q_send.shape[1:])

    q_copies = []
    for j in range(1, tensor):
        other = shift(t, j, tensor)
        q_send[other] = packed(other)
        copy = pltpu.make_async_remote_copy(
            src_ref=q_send.at[other],
            dst_ref=q_recv.at[t],
            send_sem=q_send_sem.at[j],
            recv_sem=q_recv_sem.at[t],
            device_id={"tensor": other},
            device_id_type=MESH,
        )
        q_copies.append(copy)
    q_recv[t] = packed(t)

    load_pin.wait()
    ins = jnp.zeros((rank, x_v.shape[0]), jnp.float32)
    for c in range(x_chunks):
        x_loads[c].wait()
        cols = slice(c * x_width, (c + 1) * x_width)
        ins += dot_nt(pin_v[:, cols], x_v[:, cols])
    load_left.wait()
    load_right.wait()
    for j in range(1, tensor):
        source = shift(t, j, tensor)
        pltpu.make_async_remote_copy(
            src_ref=outs.at[source],
            dst_ref=outs.at[source],
            send_sem=a_send_sem.at[j],
            recv_sem=a_recv_sem.at[source],
            device_id={"tensor": source},
            device_id_type=MESH,
        ).wait_recv()
    grads = jnp.zeros((rank, rank), jnp.float32)
    for j in range(tensor):
        grads += dot_nt(outs[j], ins[:, j * own_tok : (j + 1) * own_tok], HIGHEST)
    half = jnp.dot(left_v[...], grads, precision=HIGHEST, preferred_element_type=jnp.float32)
    block = jnp.dot(half, right_v[...], precision=HIGHEST, preferred_element_type=jnp.float32)
    block = block.reshape(tensor, 2, pairs, rank)
    p_send[...] = jnp.concatenate([block[:, 0], block[:, 1]], axis=-1)

    b_copies = []
    for i, j in block_peers:
        other = shift(t, j, tensor)
        copy = pltpu.make_async_remote_copy(
            src_ref=p_send,
            dst_ref=p_recv.at[d, t],
            send_sem=b_send_sem.at[i, j],
            recv_sem=b_recv_sem.at[d, t],
            device_id={"dp": shift(d, i, dp), "tensor": other},
            device_id_type=MESH,
        )
        copy.start()
        b_copies.append(copy)
    for copy in q_copies:
        copy.start()
    p_recv[d, t] = p_send[...]
    for j in range(1, tensor):
        source = shift(t, j, tensor)
        pltpu.make_async_remote_copy(
            src_ref=q_send.at[source],
            dst_ref=q_recv.at[source],
            send_sem=q_send_sem.at[j],
            recv_sem=q_recv_sem.at[source],
            device_id={"tensor": source},
            device_id_type=MESH,
        ).wait_recv()
    for i, j in block_peers:
        from_d, from_t = shift(d, i, dp), shift(t, j, tensor)
        pltpu.make_async_remote_copy(
            src_ref=p_send,
            dst_ref=p_recv.at[from_d, from_t],
            send_sem=b_send_sem.at[i, j],
            recv_sem=b_recv_sem.at[from_d, from_t],
            device_id={"dp": from_d, "tensor": from_t},
            device_id_type=MESH,
        ).wait_recv()
    precond = p_recv[:, 0]
    for j in range(1, tensor):
        precond += p_recv[:, j]
    lanes = dp * pairs
    products = jnp.zeros((pipe * nq * pairs, lanes), jnp.float32)
    for j in range(tensor):
        share = precond[:, j].reshape(lanes, 2 * rank).astype(jnp.bfloat16)
        products += dot_nt(q_recv[j], share)
    products = products.reshape(pipe * nq, pairs, lanes)
    row = lax.broadcasted_iota(jnp.int32, (pairs, lanes), 0)
    lane = lax.broadcasted_iota(jnp.int32, (pairs, lanes), 1)
    same = (lax.rem(lane, pairs) == row)[None]
    sums = jnp.sum(jnp.where(same, products, 0.0), axis=1)
    s_send[...] = sums.reshape(s_send.shape)

    c_copies = []
    for i in range(1, pipe):
        other = shift(p, i, pipe)
        copy = pltpu.make_async_remote_copy(
            src_ref=s_send.at[other],
            dst_ref=s_recv.at[p],
            send_sem=c_send_sem.at[i],
            recv_sem=c_recv_sem.at[p],
            device_id={"pipe": other},
            device_id_type=MESH,
        )
        copy.start()
        c_copies.append(copy)
    s_recv[p] = s_send[p]
    for i in range(1, pipe):
        source = shift(p, i, pipe)
        pltpu.make_async_remote_copy(
            src_ref=s_send.at[source],
            dst_ref=s_recv.at[source],
            send_sem=c_send_sem.at[i],
            recv_sem=c_recv_sem.at[source],
            device_id={"pipe": source},
            device_id_type=MESH,
        ).wait_recv()
    scores = s_recv[0]
    for i in range(1, pipe):
        scores += s_recv[i]
    owner = lax.broadcasted_iota(jnp.int32, (dp, lanes), 0)
    lane = lax.broadcasted_iota(jnp.int32, (dp, lanes), 1)
    gather = jnp.where(lax.div(lane, pairs) == owner, 1.0, 0.0).astype(jnp.float32)
    out_ref[...] = dot_nt(gather, scores, HIGHEST)
    for copy in a_copies + b_copies + q_copies + c_copies:
        copy.wait_send()


def cut(width):
    return max(n for n in (1, 2, 3, 4) if width % (n * 128) == 0)


def local(mesh, *args):
    x, g, pin, pout, counts, mask, left, right, queries, query_ids = args
    dp, pipe, tensor = mesh.shape["dp"], mesh.shape["pipe"], mesh.shape["tensor"]
    rank = pin.shape[1]
    rows = rank // tensor
    nq = queries.shape[0]
    parts = pipe * tensor
    lanes = dp * rows // 2
    x_chunks, g_chunks = cut(x.shape[2]), cut(g.shape[2])
    f32, bf16 = jnp.float32, jnp.bfloat16
    hbm = pl.BlockSpec(memory_space=pltpu.HBM)
    dma = pltpu.SemaphoreType.DMA
    scores = pl.pallas_call(
        functools.partial(kernel, (dp, pipe, tensor, x_chunks, g_chunks)),
        out_shape=jax.ShapeDtypeStruct((dp, nq // parts), f32),
        in_specs=[hbm] * 9,
        out_specs=pl.BlockSpec(memory_space=pltpu.VMEM),
        scratch_shapes=[
            pltpu.VMEM(x.shape[1:], bf16),
            pltpu.VMEM(g.shape[1:], bf16),
            pltpu.VMEM(pin.shape[1:], bf16),
            pltpu.VMEM(pout.shape[1:], bf16),
            pltpu.SMEM(counts.shape, jnp.int32),
            pltpu.VMEM((1, mask.shape[0]), jnp.int32),
            pltpu.VMEM((rank, rank), f32),
            pltpu.VMEM((rank, rank), f32),
            pltpu.VMEM((nq, rows, rank), bf16),
            pltpu.VMEM((tensor, pipe * (nq // parts) * rows // 2, 2 * rank), bf16),
            pltpu.VMEM((tensor, pipe * (nq // parts) * rows // 2, 2 * rank), bf16),
            pltpu.VMEM((tensor, rank, g.shape[1]), f32),
            pltpu.VMEM((tensor, rows // 2, 2 * rank), f32),
            pltpu.VMEM((dp, tensor, tensor, rows // 2, 2 * rank), f32),
            pltpu.VMEM((pipe, nq // parts, lanes), f32),
            pltpu.VMEM((pipe, nq // parts, lanes), f32),
            dma((7,)),
            dma((x_chunks,)),
            dma((g_chunks,)),
            dma((tensor,)),
            dma((tensor,)),
            dma((dp, tensor)),
            dma((dp, tensor)),
            dma((tensor,)),
            dma((tensor,)),
            dma((pipe,)),
            dma((pipe,)),
        ],
        compiler_params=pltpu.CompilerParams(
            collective_id=0, has_side_effects=True, vmem_limit_bytes=60 * 1024 * 1024
        ),
        name="attribution",
    )(x, g, pin, pout, counts, mask.reshape(1, -1), left, right, queries)
    hits = query_ids[None, :] == jnp.arange(dp, dtype=jnp.int32)[:, None]
    return jnp.where(hits, 0.0, scores).T


def solution(mesh):
    placed = (
        P("pipe", ("groups", "dp"), "tensor"),
        P("pipe", ("groups", "dp", "tensor"), None),
        P("pipe", None, "tensor"),
        P("pipe", None, None),
        P(("groups", "dp")),
        P(("groups", "dp")),
        P("pipe", None, None),
        P("pipe", None, None),
        P("dp", "pipe", "tensor", None),
        P(("groups", "dp", "pipe", "tensor")),
    )
    return jax.shard_map(
        functools.partial(local, mesh),
        mesh=mesh,
        in_specs=placed,
        out_specs=P(("dp", "pipe", "tensor"), "groups"),
        check_vma=False,
    )
```
